512 devices in a mesh: section: 4 (over x), shard: 128 (over y, z, core).
Axes of the slice: x: 4, y: 4, z: 16, core: 2. Of those that a mesh axis runs over, the one named last changes fastest.
Arguments:
- memory: bfloat16 [131072, 512], P('shard'), may hold values from -6 to 6
- messages: bfloat16 [2, 128, 128, 4, 512], P(None, 'shard', None, 'section'), may hold values from -6 to 6
- slot_rows: int32 [2, 128, 128, 4], P(None, 'shard', None, 'section'), may hold values from 0 to 1023, as said below
- counts: int32 [2, 128, 128], P(None, 'shard'), may hold values from 0 to 4, as said below
- src_slot: int32 [2, 65536], P(None, ('section', 'shard')), may hold values from 0 to 127
- nbr_slots: int32 [2, 65536, 10], P(None, ('section', 'shard')), may hold values from 0 to 127
- time_gap: float32 [2, 65536, 10], P(None, ('section', 'shard')), may hold values from 0.1 to 100
- time_freq: float32 [128], replicated, may hold values from 0.01 to 1
- time_phase: float32 [128], replicated, may hold values from -3.140625 to 3.140625
- gru_input: bfloat16 [512, 1536], P('section'), may hold values from -0.25 to 0.25
- gru_hidden: bfloat16 [512, 1536], P('section'), may hold values from -0.25 to 0.25
- gru_bias: float32 [2, 1536], replicated, may hold values from -3 to 3
- attn_qkv: bfloat16 [512, 1536], P('section'), may hold values from -0.25 to 0.25
- attn_out: bfloat16 [512, 512], P('section'), may hold values from -0.25 to 0.25
- time_proj: bfloat16 [128, 1024], P('section'), may hold values from -0.5 to 0.5
Outputs:
- memory_out: bfloat16 [131072, 512], P('shard')
- embeddings: bfloat16 [2, 65536, 512], P(None, ('section', 'shard'))
The draws below stay inside these ranges and needn't reach their ends.
Inputs may be any that keep to these rules, and one draw needn't show every extreme that they name: `slot_rows`: within one batch the rows of one owner named by all devices' slots are distinct. `counts`: in every batch one owner receives 4 live slots from every device.
All inputs are finite; a program needn't handle non-finite values.
Results may differ from the reference program's by a relative error of at most 0.015.
Values may be sent and summed in bfloat16 or wider, within the bound.
No kernel may reach another device: no remote copies, remote signals or barrier semaphores. Data moves between devices by JAX's collectives and lax.ppermute only.
A program may use at most 128 MiB of HBM per device.

```python
import math
import jax
import jax.numpy as jnp
from jax import lax

F = 512
TE = 128
HEADS = 2
HD = 256
NBR = 10
CAP = 4
BATCHES = 2
NODES_DEV = 1024
EV_DEV = 128
NODES = 131072
EVENTS = 65536
POOL = 128
N_SECTION = 4
N_SHARD = 128


def draw_slot_rows(key, part):
    key = jax.random.fold_in(key, 11)
    marks = jax.random.randint(key, (BATCHES, N_SHARD, NODES_DEV), 0, 2 ** 16)
    scores = marks * NODES_DEV + jnp.arange(NODES_DEV, dtype=jnp.int32)[None, None, :]
    order = jnp.argsort(scores, axis=-1, stable=True).astype(jnp.int32)
    taken = order[:, :, :N_SHARD * CAP].reshape(BATCHES, N_SHARD, N_SHARD, CAP)
    return jnp.transpose(taken, (0, 2, 1, 3)).astype(jnp.int32)


def draw_counts(key, part):
    key = jax.random.fold_in(key, 23)
    first, second, third = jax.random.split(key, 3)
    ceiling = jax.random.randint(first, (BATCHES, 1, N_SHARD), 1, 2 * CAP + 1)
    raw = jax.random.randint(second, (BATCHES, N_SHARD, N_SHARD), 0, 2 ** 16) % ceiling
    loads = jnp.minimum(raw, CAP)
    busy = jax.random.randint(third, (BATCHES, 1, 1), 0, N_SHARD)
    full = jnp.arange(N_SHARD, dtype=jnp.int32)[None, None, :] == busy
    return jnp.where(full, CAP, loads).astype(jnp.int32)


def set_ends(drawn, own_key, least, high):
    longest = drawn.shape.index(max(drawn.shape))
    spots = []
    for shift in (0, 1):
        where = [jax.random.randint(jax.random.fold_in(own_key, axis), (), 0, length) for axis, length in enumerate(drawn.shape)]
        where[longest] = (where[longest] + shift) % drawn.shape[longest]
        spots.append(tuple(where))
    return drawn.at[spots[0]].set(least).at[spots[1]].set(high)


def level_of(rng, extent, cuts, smallest, largest):
    def one(position, shards_of):
        draws = jax.random.uniform(jax.random.fold_in(jax.random.fold_in(rng, 6), position), (shards_of,), jnp.float32, smallest / len(cuts), largest / len(cuts))
        return jnp.repeat(jnp.exp(draws), extent[position] // shards_of).reshape((-1,) + (1,) * (len(extent) - position - 1))

    factor_of = one(*cuts[0])
    for cut in cuts[1:]:
        factor_of = factor_of * one(*cut)
    return factor_of


def normal_values(key, dims, deviation, limit, cuts=(), kind=jnp.bfloat16):
    level = level_of(key, dims, cuts, -0.22, 0.18) if cuts else 1.0
    drawn = jax.random.normal(key, dims, jnp.float32) * deviation * level
    return jnp.minimum(jnp.maximum(drawn, -limit), limit).astype(kind)


def setup_inputs(seed: int = 0) -> dict:
    streams_of = jax.random.split(jax.random.key(seed), 16)
    return {
        "memory": normal_values(streams_of[0], (NODES, F), 1.0, 6.0, ((0, 128),)),
        "messages": normal_values(streams_of[1], (BATCHES, N_SHARD, N_SHARD, CAP, F), 1.0, 6.0, ((1, 128), (3, 4))),
        "slot_rows": draw_slot_rows(jax.random.fold_in(streams_of[15], 71), 0),
        "counts": draw_counts(jax.random.fold_in(streams_of[15], 71), 0),
        "src_slot": set_ends(jax.random.randint(streams_of[4], (BATCHES, EVENTS), 0, POOL), jax.random.fold_in(streams_of[4], 1), 0, POOL - 1).astype(jnp.int32),
        "nbr_slots": set_ends(jax.random.randint(streams_of[5], (BATCHES, EVENTS, NBR), 0, POOL), jax.random.fold_in(streams_of[5], 1), 0, POOL - 1).astype(jnp.int32),
        "time_gap": jnp.clip(jnp.exp(math.log(100.0) - 6.9077553 * jax.random.uniform(streams_of[6], (BATCHES, EVENTS, NBR), jnp.float32) ** level_of(streams_of[6], (BATCHES, EVENTS, NBR), ((1, 512),), -0.2, 0.2)), 0.1, 100.0),
        "time_freq": jnp.clip(jnp.exp(jax.random.uniform(streams_of[7], (TE,), jnp.float32, math.log(0.01), math.log(1.0))), 0.01, 1.0),
        "time_phase": jnp.clip(jax.random.uniform(streams_of[8], (TE,), jnp.float32, -3.140625, 3.140625), -3.140625, 3.140625),
        "gru_input": normal_values(streams_of[9], (F, 3 * F), F ** -0.5, 0.25, ((0, 4),)),
        "gru_hidden": normal_values(streams_of[10], (F, 3 * F), F ** -0.5, 0.25, ((0, 4),)),
        "gru_bias": normal_values(streams_of[11], (2, 3 * F), 0.5, 3.0, (), jnp.float32),
        "attn_qkv": normal_values(streams_of[12], (F, 3 * F), F ** -0.5, 0.25, ((0, 4),)),
        "attn_out": normal_values(streams_of[13], (F, F), F ** -0.5, 0.25, ((0, 4),)),
        "time_proj": normal_values(streams_of[14], (TE, 2 * F), TE ** -0.5, 0.5, ((0, 4),)),
    }


def gru_rows(x, h, w_in, w_hid, bias):
    width = x.shape[1]
    gx = jnp.dot(x, w_in, preferred_element_type=jnp.float32) + bias[0]
    gh = jnp.dot(h, w_hid, preferred_element_type=jnp.float32) + bias[1]
    reset = jax.nn.sigmoid(gx[:, :width] + gh[:, :width])
    update = jax.nn.sigmoid(gx[:, width:2 * width] + gh[:, width:2 * width])
    fresh = jnp.tanh(gx[:, 2 * width:] + reset * gh[:, 2 * width:])
    return ((1.0 - update) * fresh + update * h.astype(jnp.float32)).astype(jnp.bfloat16)

def embed(pool, source, nearby, gaps, freq, phase, qkv, out_w, tproj):
    width = pool.shape[1]
    events = source.shape[0]
    kv = jnp.dot(pool, qkv[:, width:], preferred_element_type=jnp.float32).astype(jnp.bfloat16)
    query = jnp.dot(pool[source], qkv[:, :width], preferred_element_type=jnp.float32)
    encoded = jnp.cos(gaps[..., None] * freq + phase).astype(jnp.bfloat16)
    timed = jnp.einsum('ent,tc->enc', encoded.astype(jnp.float32), tproj.astype(jnp.float32))
    near = kv[nearby].astype(jnp.float32) + timed
    keys = near[..., :width].reshape(events, NBR, HEADS, HD)
    values = near[..., width:].reshape(events, NBR, HEADS, HD)
    scores = jnp.einsum('ehd,enhd->ehn', query.reshape(events, HEADS, HD), keys) / jnp.sqrt(jnp.float32(HD))
    weights = jax.nn.softmax(scores, axis=-1)
    mixed = jnp.einsum('ehn,enhd->ehd', weights, values).reshape(events, width).astype(jnp.bfloat16)
    return jnp.dot(mixed, out_w, preferred_element_type=jnp.float32).astype(jnp.bfloat16)

def reference(memory, messages, slot_rows, counts, src_slot, nbr_slots, time_gap, time_freq, time_phase, gru_input, gru_hidden, gru_bias, attn_qkv, attn_out, time_proj):
    quarter = CAP // N_SECTION
    devices = N_SECTION * N_SHARD
    owners = jnp.arange(N_SHARD, dtype=jnp.int32)
    slots = jnp.arange(CAP, dtype=jnp.int32)
    outputs = []
    for batch in range(BATCHES):
        live = slots[None, None, :] < counts[batch][:, :, None]
        node = owners[None, :, None] * NODES_DEV + slot_rows[batch]
        fetched = jnp.where(live[..., None], memory[node], jnp.zeros((), jnp.bfloat16))

        def one_source(pair):
            return gru_rows(pair[0], pair[1], gru_input, gru_hidden, gru_bias)
        updated = lax.map(one_source, (messages[batch].reshape(N_SHARD, N_SHARD * CAP, F), fetched.reshape(N_SHARD, N_SHARD * CAP, F)))
        updated = updated.reshape(N_SHARD, N_SHARD, CAP, F)
        target = jnp.where(live, node, NODES).reshape(-1)
        memory = memory.at[target].set(updated.reshape(-1, F), mode='drop')
        pools = updated.reshape(N_SHARD, N_SHARD, N_SECTION, quarter, F).transpose(2, 0, 1, 3, 4).reshape(devices, POOL, F)

        def one_device(items):
            return embed(items[0], items[1], items[2], items[3], time_freq, time_phase, attn_qkv, attn_out, time_proj)
        result = lax.map(one_device, (pools, src_slot[batch].reshape(devices, EV_DEV), nbr_slots[batch].reshape(devices, EV_DEV, NBR), time_gap[batch].reshape(devices, EV_DEV, NBR)))
        outputs.append(result.reshape(EVENTS, F))
    return (memory, jnp.stack(outputs))
```

```python
import functools
import math

import jax
import jax.numpy as jnp
from jax import lax
from jax.experimental import pallas as pl
from jax.experimental.pallas import tpu as pltpu
from jax.sharding import PartitionSpec as P

HEADS = 2
HD = 256
BATCHES = 2
NBR = 10
F = 512
TE = 128
G = 3 * F
DIGIT = 32
EXTRA = 16
HALF = 2688
BF = jnp.bfloat16
F32 = jnp.float32
VMEM_LIMIT = 40 * 2**20

VSPEC = pl.BlockSpec(memory_space=pltpu.VMEM)
ASPEC = pl.BlockSpec(memory_space=pl.ANY)
SSPEC = pl.BlockSpec(memory_space=pltpu.SMEM)
PARAMS = pltpu.CompilerParams(vmem_limit_bytes=VMEM_LIMIT)


def dot(a, b):
    return jnp.dot(a, b, preferred_element_type=F32)


def dot_nt(a, b):
    return lax.dot_general(a, b, (((1,), (1,)), ((), ())), preferred_element_type=F32)


def dot_tn(a, b):
    return lax.dot_general(a, b, (((0,), (0,)), ((), ())), preferred_element_type=F32)


def split(x):
    high = x.astype(BF)
    return high, (x - high.astype(F32)).astype(BF)


def iota(shape, dim):
    return lax.broadcasted_iota(jnp.int32, shape, dim)


def hot(mask):
    return jnp.where(mask, 1.0, 0.0).astype(BF)


TWO_PI_HIGH = 6.28125
TWO_PI_LOW = 2.0 * math.pi - TWO_PI_HIGH
SERIES = [(-1.0) ** k / math.factorial(2 * k) for k in range(9)]


def cosine(x):
    turns = jnp.round(x * (1.0 / (2.0 * math.pi)))
    r = (x - turns * TWO_PI_HIGH) - turns * TWO_PI_LOW
    s = r * r
    y = jnp.full_like(s, SERIES[8])
    for k in range(7, -1, -1):
        y = y * s + SERIES[k]
    return y


def encode_kernel(gap, freq, phase, te):
    for b in range(BATCHES):
        for n in range(NBR):
            te[b, n] = cosine(freq[...] * gap[b, n : n + 1, :] + phase[...]).astype(BF)


def place_kernel(pos, mine, other, w_in, w_hid, w_qkv, w_out, w_time, sems):
    section = pos[1]

    def copies(first, second):
        found = []
        for j in range(4):
            at = pl.multiple_of(((section - j + 4) % 4) * 128, 128)
            rows = pl.ds(at, 128)
            found += [
                (first.at[j, :, pl.ds(0, G)], w_in.at[rows, :]),
                (second.at[j, :, pl.ds(0, G)], w_hid.at[rows, :]),
                (first.at[j, :, pl.ds(G, 1152)], w_qkv.at[rows, pl.ds(0, 1152)]),
                (second.at[j, :, pl.ds(G, 384)], w_qkv.at[rows, pl.ds(1152, 384)]),
                (second.at[j, :, pl.ds(1920, F)], w_out.at[rows, :]),
            ]
            time_rows = pl.ds(pl.multiple_of(((section - j + 4) % 4) * 32, 32), 32)
            for q in range(4):
                found.append(
                    (
                        second.at[j, pl.ds(32 * q, 32), pl.ds(2432, 256)],
                        w_time.at[time_rows, pl.ds(256 * q, 256)],
                    )
                )
        return found

    def move(first, second):
        started = []
        for i, (source, target) in enumerate(copies(first, second)):
            copy = pltpu.make_async_copy(source, target, sems.at[i])
            copy.start()
            started.append(copy)
        for copy in started:
            copy.wait()

    @pl.when(pos[0] == 0)
    def _():
        move(mine, other)

    @pl.when(pos[0] != 0)
    def _():
        move(other, mine)


def gates(gx, gh, h):
    reset = jax.nn.sigmoid(gx[:, :F] + gh[:, :F])
    update = jax.nn.sigmoid(gx[:, F : 2 * F] + gh[:, F : 2 * F])
    fresh = jnp.tanh(gx[:, 2 * F :] + reset * gh[:, 2 * F :])
    return ((1.0 - update) * fresh + update * h.astype(F32)).astype(BF)


def first_kernel(recv, memory, w_in, w_hid, bias, up, gx1, base):
    slots = recv.shape[0]
    rows = memory.shape[0]
    digits = recv[:, 2 * F : 2 * F + 128].astype(F32)
    up[slots:, :] = jnp.zeros((EXTRA, F), BF)
    up[slots:, :slots] = digits.T[:EXTRA, :].astype(BF)
    number = iota((slots, rows), 1).astype(F32)
    hot0 = hot(number == digits[:, 0:1] * DIGIT + digits[:, 1:2])
    hot1 = hot(number == digits[:, 2:3] * DIGIT + digits[:, 3:4])
    got = dot(jnp.concatenate([hot0, hot1], axis=0), memory[...]).astype(BF)
    base[...] = got[slots:]
    sent = jnp.concatenate([recv[:, :F], recv[:, F : 2 * F]], axis=0)
    gx = dot(sent, w_in[...]) + bias[0:1, :]
    gx1[...] = gx[slots:]
    h = got[:slots]
    gh = dot(h, w_hid[...]) + bias[1:2, :]
    up[:slots, :] = gates(gx[:slots], gh, h)


def numbers(ups, batch, slots):
    parts = []
    for t in range(ups.shape[0] // (slots + EXTRA)):
        at = t * (slots + EXTRA) + slots
        pair = ups[at : at + EXTRA, :slots].astype(F32)
        parts.append(pair[2 * batch : 2 * batch + 1] * DIGIT + pair[2 * batch + 1 : 2 * batch + 2])
    return jnp.concatenate(parts, axis=1)


def values(ups, slots):
    parts = []
    for t in range(ups.shape[0] // (slots + EXTRA)):
        at = t * (slots + EXTRA)
        parts.append(ups[at : at + slots, :])
    return jnp.concatenate(parts, axis=0)


def second_kernel(dead, recv, ups, gx1, base, w_hid, bias, up):
    slots = recv.shape[0]
    digits = recv[:, 2 * F : 2 * F + 128].astype(F32)
    mine = digits[:, 2:3] * DIGIT + digits[:, 3:4]
    same = (numbers(ups, 0, slots) == mine) & (mine < dead)
    any_same = jnp.max(jnp.where(same, 1.0, 0.0), axis=1, keepdims=True)
    moved = dot(hot(same), values(ups, slots))
    h = jnp.where(any_same > 0.0, moved, base[...].astype(F32)).astype(BF)
    gh = dot(h, w_hid[...]) + bias[1:2, :]
    up[...] = gates(gx1[...], gh, h)


def store_kernel(memory, ups0, ups1, out):
    block = memory.shape[0]
    slots = ups0.shape[0] // (ups1.shape[0] // 128) - EXTRA
    number = (iota((block, 1), 0) + pl.program_id(0) * block).astype(F32)
    hot0 = hot(numbers(ups0, 0, slots) == number)
    hot1 = hot(numbers(ups0, 1, slots) == number)
    ones = jnp.ones((hot0.shape[1], 128), BF)
    seen0, seen1 = dot(hot0, ones), dot(hot1, ones)
    new0 = dot(hot0, values(ups0, slots))
    new1 = dot(hot1, ups1[...])
    for c in range(0, F, 128):
        cols = slice(c, c + 128)
        old = jnp.where(seen0 > 0.0, new0[:, cols], memory[:, cols].astype(F32))
        out[:, cols] = jnp.where(seen1 > 0.0, new1[:, cols], old).astype(BF)


def attend_kernel(pools, source, nearby, te, w_qkv, w_out, w_time, out):
    slots = pools.shape[0]
    events = source.shape[1]
    number = iota((slots, events), 0)
    for b in range(BATCHES):
        pool = pools[:, b * F : (b + 1) * F]
        kv = dot(pool, w_qkv[:, F:]).astype(BF)
        picked = dot_tn(hot(number == source[b : b + 1, :]), pool).astype(BF)
        query = dot(picked, w_qkv[:, :F]) * (1.0 / math.sqrt(HD))
        hits = [number == nearby[b, n : n + 1, :] for n in range(NBR)]
        near_te = [te[b, n].astype(F32) for n in range(NBR)]
        pieces = []
        for head in range(HEADS):
            cols = slice(head * HD, (head + 1) * HD)
            vcols = slice(F + head * HD, F + (head + 1) * HD)
            high, low = split(query[:, cols])
            by_slot = dot_nt(kv[:, cols], high) + dot_nt(kv[:, cols], low)
            by_time = dot_nt(w_time[:, cols], high) + dot_nt(w_time[:, cols], low)
            scores = [
                jnp.sum(
                    jnp.where(hits[n], by_slot, 0.0) + by_time * near_te[n],
                    axis=0,
                    keepdims=True,
                )
                for n in range(NBR)
            ]
            top = functools.reduce(jnp.maximum, scores)
            grown = [jnp.exp(s - top) for s in scores]
            scale = 1.0 / functools.reduce(jnp.add, grown)
            on_slot = jnp.zeros((slots, events), F32)
            on_time = jnp.zeros((TE, events), F32)
            for n in range(NBR):
                weight = grown[n] * scale
                on_slot = on_slot + jnp.where(hits[n], weight, 0.0)
                on_time = on_time + near_te[n] * weight
            s_high, s_low = split(on_slot)
            t_high, t_low = split(on_time)
            pieces.append(
                dot_tn(s_high, kv[:, vcols])
                + dot_tn(s_low, kv[:, vcols])
                + dot_tn(t_high, w_time[:, vcols])
                + dot_tn(t_low, w_time[:, vcols])
            )
        mixed = jnp.concatenate(pieces, axis=1).astype(BF)
        out[b] = dot(mixed, w_out[...]).astype(BF)


def call(kernel, n_in, outs, flops, args, name, **more):
    many = isinstance(outs, (list, tuple))
    moved = sum(a.size * a.dtype.itemsize for a in args)
    return pl.pallas_call(
        kernel,
        out_shape=outs,
        in_specs=more.pop("in_specs", [VSPEC] * n_in),
        out_specs=more.pop("out_specs", [VSPEC] * len(outs) if many else VSPEC),
        compiler_params=PARAMS,
        cost_estimate=pl.CostEstimate(flops=flops, bytes_accessed=moved, transcendentals=0),
        name=name,
        **more,
    )(*args)


def shape(dims, kind):
    return jax.ShapeDtypeStruct(dims, kind)


def body(
    memory,
    messages,
    slot_rows,
    counts,
    src_slot,
    nbr_slots,
    time_gap,
    time_freq,
    time_phase,
    gru_input,
    gru_hidden,
    gru_bias,
    attn_qkv,
    attn_out,
    time_proj,
):
    rows = memory.shape[0]
    slots = slot_rows.shape[2]
    events = src_slot.shape[1]
    section = lax.axis_index("section")
    core = lax.axis_index("shard") % 2
    sections = lax.axis_size("section")
    shards = lax.axis_size("shard")

    times = time_proj.reshape(32, 4, 256).transpose(1, 0, 2).reshape(128, 256)
    first = jnp.concatenate([gru_input, attn_qkv[:, :1152]], axis=1)
    second = jnp.concatenate([gru_hidden, attn_qkv[:, 1152:], attn_out, times], axis=1)
    half = jnp.where(core == 0, first, second)
    parts = [half] + [
        lax.ppermute(half, "section", [(i, (i + k) % sections) for i in range(sections)])
        for k in range(1, sections)
    ]
    mine = jnp.stack(parts)
    other = lax.ppermute(mine, "shard", [(i, i ^ 1) for i in range(shards)])

    alive = section < counts[:, 0]
    wanted = jnp.where(alive, slot_rows[:, 0, :, 0], rows)
    digits = jnp.stack(
        [wanted[0] // DIGIT, wanted[0] % DIGIT, wanted[1] // DIGIT, wanted[1] % DIGIT], axis=1
    ).astype(BF)
    sent = jnp.concatenate(
        [
            messages[0, 0, :, 0],
            messages[1, 0, :, 0],
            digits,
            jnp.zeros((slots, 128 - 4), BF),
        ],
        axis=1,
    )
    recv = lax.all_to_all(sent, "shard", split_axis=0, concat_axis=0, tiled=True)

    te = call(
        encode_kernel,
        3,
        shape((BATCHES, NBR, TE, events), BF),
        10**7,
        (time_gap.transpose(0, 2, 1), time_freq.reshape(TE, 1), time_phase.reshape(TE, 1)),
        "encode",
    )
    pos = jnp.stack([core, section]).astype(jnp.int32)
    w_in, w_hid, w_qkv, w_out, w_time = call(
        place_kernel,
        3,
        [shape((F, G), BF), shape((F, G), BF), shape((F, G), BF), shape((F, F), BF), shape((TE, 2 * F), BF)],
        0,
        (pos, mine, other),
        "place",
        in_specs=[SSPEC, ASPEC, ASPEC],
        out_specs=[ASPEC] * 5,
        scratch_shapes=[pltpu.SemaphoreType.DMA((36,))],
    )

    up0, gx1, base = call(
        first_kernel,
        5,
        [shape((slots + EXTRA, F), BF), shape((slots, G), F32), shape((slots, F), BF)],
        10**9,
        (recv, memory, w_in, w_hid, gru_bias),
        "first_batch",
    )
    ups0 = lax.all_gather(up0, "section", axis=0, tiled=True)
    up1 = call(
        functools.partial(second_kernel, float(rows)),
        6,
        shape((slots, F), BF),
        3 * 10**8,
        (recv, ups0, gx1, base, w_hid, gru_bias),
        "second_batch",
    )
    pools = lax.all_to_all(
        jnp.concatenate([up0[:slots], up1], axis=1), "shard", split_axis=0, concat_axis=0, tiled=True
    )
    ups1 = lax.all_gather(up1, "section", axis=0, tiled=True)
    memory_out = call(
        store_kernel,
        3,
        shape((rows, F), BF),
        10**9,
        (memory, ups0, ups1),
        "store",
        grid=(4,),
        in_specs=[
            pl.BlockSpec((rows // 4, F), lambda i: (i, 0)),
            pl.BlockSpec(ups0.shape, lambda i: (0, 0)),
            pl.BlockSpec(ups1.shape, lambda i: (0, 0)),
        ],
        out_specs=pl.BlockSpec((rows // 4, F), lambda i: (i, 0)),
    )
    embeddings = call(
        attend_kernel,
        7,
        shape((BATCHES, events, F), BF),
        10**9,
        (pools, src_slot, nbr_slots.transpose(0, 2, 1), te, w_qkv, w_out, w_time),
        "attend",
    )
    return memory_out, embeddings


def solution(mesh):
    in_specs = (
        P("shard", None),
        P(None, "shard", None, "section", None),
        P(None, "shard", None, "section"),
        P(None, "shard", None),
        P(None, ("section", "shard")),
        P(None, ("section", "shard"), None),
        P(None, ("section", "shard"), None),
        P(),
        P(),
        P("section", None),
        P("section", None),
        P(),
        P("section", None),
        P("section", None),
        P("section", None),
    )
    out_specs = (P("shard", None), P(None, ("section", "shard"), None))
    return jax.shard_map(body, mesh=mesh, in_specs=in_specs, out_specs=out_specs, check_vma=False)
```

```python
import functools
import math

import jax
import jax.numpy as jnp
from jax import lax
from jax.experimental import pallas as pl
from jax.experimental.pallas import tpu as pltpu
from jax.sharding import Mesh
from jax.sharding import PartitionSpec as P

HEADS = 2
HD = 256
BATCHES = 2
NBR = 10
F = 512
TE = 128
G = 3 * F
DIGIT = 32
EXTRA = 16
SHARD = ("chip", "core")
ALL = ("section", "chip", "core")
BF = jnp.bfloat16
F32 = jnp.float32
VMEM_LIMIT = 40 * 2**20
WIDE = 2 * G + G + F + 256
PACK_LIMIT = 56 * 2**20

SECTIONS = 4
HSPEC = pl.BlockSpec(memory_space=pltpu.HBM)
VSPEC = pl.BlockSpec(memory_space=pltpu.VMEM)


def dot(a, b):
    return jnp.dot(a, b, preferred_element_type=F32)


def dot_nt(a, b):
    return lax.dot_general(a, b, (((1,), (1,)), ((), ())), preferred_element_type=F32)


def dot_tn(a, b):
    return lax.dot_general(a, b, (((0,), (0,)), ((), ())), preferred_element_type=F32)


def split(x):
    high = x.astype(BF)
    return high, (x - high.astype(F32)).astype(BF)


def iota(shape, dim):
    return lax.broadcasted_iota(jnp.int32, shape, dim)


def hot(mask):
    return jnp.where(mask, 1.0, 0.0).astype(BF)


TWO_PI_HIGH = 6.28125
TWO_PI_LOW = 2.0 * math.pi - TWO_PI_HIGH
SERIES = [(-1.0) ** k / math.factorial(2 * k) for k in range(9)]


def cosine(x):
    turns = jnp.round(x * (1.0 / (2.0 * math.pi)))
    r = (x - turns * TWO_PI_HIGH) - turns * TWO_PI_LOW
    s = r * r
    y = jnp.full_like(s, SERIES[8])
    for k in range(7, -1, -1):
        y = y * s + SERIES[k]
    return y


def encode(gap, freq, phase, te):
    events = gap.shape[2]
    speed = jnp.broadcast_to(freq[...], (events, TE)).T
    start = jnp.broadcast_to(phase[...], (events, TE)).T
    for b in range(BATCHES):
        for n in range(NBR):
            te[b, n] = cosine(speed * gap[b, n : n + 1, :] + start).astype(BF)


def pack_kernel(dead, counts, wanted, messages, w_in, w_hid, w_qkv, w_out, w_time, sent, bundle, sems):
    pairs = []
    for array, at, width in [(w_in, 0, G), (w_hid, G, G), (w_qkv, 2 * G, G), (w_out, 3 * G, F)]:
        pairs.append((array, bundle.at[:, pl.ds(at, width)]))
    rows = w_time.shape[0]
    for q in range(4):
        piece = w_time.at[:, pl.ds(256 * q, 256)]
        pairs.append((piece, bundle.at[pl.ds(rows * q, rows), pl.ds(3 * G + F, 256)]))
    started = []
    for i, (source, target) in enumerate(pairs):
        copy = pltpu.make_async_copy(source, target, sems.at[i])
        copy.start()
        started.append(copy)
    number = jnp.where(counts[...] > lax.axis_index("section"), wanted[...], dead)
    high = (number // DIGIT).astype(F32)
    low = (number % DIGIT).astype(F32)
    lines = [high[0:1], low[0:1], high[1:2], low[1:2], jnp.zeros((124, number.shape[1]), F32)]
    digits = jnp.concatenate(lines, axis=0).T.astype(BF)
    for b in range(BATCHES):
        sent[:, b, :F] = messages[b]
        sent[:, b, F:] = digits
    wait(started)


def copies(pieces, col, width, target, sems):
    own, beside, across, far, far_across = pieces
    core, section = lax.axis_index("core"), lax.axis_index("section")
    count, half = own.shape[0], far.shape[0]
    turn = 1 - 2 * core
    started = []

    def put(source, step, first, length):
        where = (section + step + SECTIONS) % SECTIONS
        rows = pl.ds(pl.multiple_of(where * count + first, half), length)
        copy = pltpu.make_async_copy(source.at[:, pl.ds(col, width)], target.at[rows, :], sems.at[len(started)])
        copy.start()
        started.append(copy)

    put(own, 0, 0, count)
    put(beside, turn, 0, count)
    put(across, -turn, 0, count)
    put(far, 2, core * half, half)
    put(far_across, 2, half - core * half, half)
    return started


def wait(started):
    for copy in started:
        copy.wait()


def gates(gx, gh, h):
    reset = jax.nn.sigmoid(gx[:, :F] + gh[:, :F])
    update = jax.nn.sigmoid(gx[:, F : 2 * F] + gh[:, F : 2 * F])
    fresh = jnp.tanh(gx[:, 2 * F :] + reset * gh[:, 2 * F :])
    return ((1.0 - update) * fresh + update * h.astype(F32)).astype(BF)


def fetch_kernel(recv, memory, got, tail):
    slots = recv.shape[0]
    rows = memory.shape[0]
    digits = recv[:, 0, F:].astype(F32)
    tail[...] = jnp.zeros((EXTRA, F), BF)
    tail[:, :slots] = digits.T[:EXTRA, :].astype(BF)
    number = iota((slots, rows), 1).astype(F32)
    hot0 = hot(number == digits[:, 0:1] * DIGIT + digits[:, 1:2])
    hot1 = hot(number == digits[:, 2:3] * DIGIT + digits[:, 3:4])
    got[...] = dot(jnp.concatenate([hot0, hot1], axis=0), memory[...]).astype(BF)


def first_kernel(recv, got, tail, bias, *rest):
    pieces, (up, gx1, w_hid, w_in, sems) = rest[:5], rest[5:]
    in_copies = copies(pieces, 0, G, w_in, sems.at[0])
    hid_copies = copies(pieces, G, G, w_hid, sems.at[1])
    slots = recv.shape[0]
    up[slots:, :] = tail[...]
    sent = jnp.concatenate([recv[:, b, :F] for b in range(BATCHES)], axis=0)
    wait(in_copies)
    gx = dot(sent, w_in[...]) + bias[0:1, :]
    gx1[...] = gx[slots:]
    h = got[:slots, :]
    wait(hid_copies)
    gh = dot(h, w_hid[...]) + bias[1:2, :]
    up[:slots, :] = gates(gx[:slots], gh, h)


def numbers(ups, batch, slots):
    parts = []
    for t in range(ups.shape[0] // (slots + EXTRA)):
        at = t * (slots + EXTRA) + slots
        pair = ups[at : at + EXTRA, :slots].astype(F32)
        parts.append(pair[2 * batch : 2 * batch + 1] * DIGIT + pair[2 * batch + 1 : 2 * batch + 2])
    return jnp.concatenate(parts, axis=1)


def values(ups, slots):
    parts = []
    for t in range(ups.shape[0] // (slots + EXTRA)):
        at = t * (slots + EXTRA)
        parts.append(ups[at : at + slots, :])
    return jnp.concatenate(parts, axis=0)


def second_kernel(dead, recv, got, ups, gx1, up0, w_hid, bias, up, both):
    slots = recv.shape[0]
    digits = recv[:, 0, F:].astype(F32)
    mine = digits[:, 2:3] * DIGIT + digits[:, 3:4]
    same = (numbers(ups, 0, slots) == mine) & (mine < dead)
    any_same = jnp.max(jnp.where(same, 1.0, 0.0), axis=1, keepdims=True)
    moved = dot(hot(same), values(ups, slots))
    h = jnp.where(any_same > 0.0, moved, got[slots:, :].astype(F32)).astype(BF)
    gh = dot(h, w_hid[...]) + bias[1:2, :]
    new = gates(gx1[...], gh, h)
    up[...] = new
    both[:, 0, :] = up0[:slots, :]
    both[:, 1, :] = new


def store_kernel(memory, ups0, ups1, out):
    block = memory.shape[0]
    slots = ups0.shape[0] // SECTIONS - EXTRA
    number = (iota((block, 1), 0) + pl.program_id(0) * block).astype(F32)
    hot0 = hot(numbers(ups0, 0, slots) == number)
    hot1 = hot(numbers(ups0, 1, slots) == number)
    ones = jnp.ones((hot0.shape[1], 128), BF)
    seen0, seen1 = dot(hot0, ones), dot(hot1, ones)
    new0 = dot(hot0, values(ups0, slots))
    new1 = dot(hot1, ups1[...])
    for c in range(0, F, 128):
        cols = slice(c, c + 128)
        old = jnp.where(seen0 > 0.0, new0[:, cols], memory[:, cols].astype(F32))
        out[:, cols] = jnp.where(seen1 > 0.0, new1[:, cols], old).astype(BF)


def attend_kernel(pools, source, nearby, gap, freq, phase, *rest):
    pieces, (out, w, bundle_time, te, sems) = rest[:5], rest[5:]
    started = copies(pieces, 2 * G, G + F, w, sems.at[0])
    started += copies(pieces, 3 * G + F, 256, bundle_time, sems.at[1])
    slots = pools.shape[0]
    events = source.shape[1]
    number = iota((slots, events), 0)
    encode(gap, freq, phase, te)
    wait(started)
    quarter = w.shape[0] // SECTIONS
    w_time = [
        jnp.concatenate([bundle_time[t * quarter + 32 * q : t * quarter + 32 * q + 32, :] for t in range(SECTIONS)], axis=0)
        for q in range(2 * HEADS)
    ]
    for b in range(BATCHES):
        pool = pools[:, b, :]
        kv = dot(pool, w[:, F:G]).astype(BF)
        picked = dot_tn(hot(number == source[b : b + 1, :]), pool).astype(BF)
        query = dot(picked, w[:, :F]) * (1.0 / math.sqrt(HD))
        hits = [number == nearby[b, n : n + 1, :] for n in range(NBR)]
        near_te = [te[b, n].astype(F32) for n in range(NBR)]
        pieces = []
        for head in range(HEADS):
            cols = slice(head * HD, (head + 1) * HD)
            vcols = slice(F + head * HD, F + (head + 1) * HD)
            high, low = split(query[:, cols])
            by_slot = dot_nt(kv[:, cols], high) + dot_nt(kv[:, cols], low)
            by_time = dot_nt(w_time[head], high) + dot_nt(w_time[head], low)
            scores = [
                jnp.sum(
                    jnp.where(hits[n], by_slot, 0.0) + by_time * near_te[n],
                    axis=0,
                    keepdims=True,
                )
                for n in range(NBR)
            ]
            top = functools.reduce(jnp.maximum, scores)
            grown = [jnp.exp(s - top) for s in scores]
            scale = 1.0 / functools.reduce(jnp.add, grown)
            on_slot = jnp.zeros((slots, events), F32)
            on_time = jnp.zeros((TE, events), F32)
            for n in range(NBR):
                weight = grown[n] * scale
                on_slot = on_slot + jnp.where(hits[n], weight, 0.0)
                on_time = on_time + near_te[n] * weight
            s_high, s_low = split(on_slot)
            t_high, t_low = split(on_time)
            pieces.append(
                dot_tn(s_high, kv[:, vcols])
                + dot_tn(s_low, kv[:, vcols])
                + dot_tn(t_high, w_time[HEADS + head])
                + dot_tn(t_low, w_time[HEADS + head])
            )
        mixed = jnp.concatenate(pieces, axis=1).astype(BF)
        out[b] = dot(mixed, w[:, G:]).astype(BF)


def call(kernel, n_in, outs, flops, args, name, **more):
    many = isinstance(outs, (list, tuple))
    moved = sum(a.size * a.dtype.itemsize for a in args)
    return pl.pallas_call(
        kernel,
        out_shape=outs,
        in_specs=more.pop("in_specs", [VSPEC] * n_in),
        out_specs=more.pop("out_specs", [VSPEC] * len(outs) if many else VSPEC),
        compiler_params=pltpu.CompilerParams(vmem_limit_bytes=more.pop("limit", VMEM_LIMIT)),
        cost_estimate=pl.CostEstimate(flops=flops, bytes_accessed=moved, transcendentals=0),
        name=name,
        **more,
    )(*args)


def shape(dims, kind):
    return jax.ShapeDtypeStruct(dims, kind)


def body(
    memory,
    messages,
    slot_rows,
    counts,
    src_slot,
    nbr_slots,
    time_gap,
    time_freq,
    time_phase,
    gru_input,
    gru_hidden,
    gru_bias,
    attn_qkv,
    attn_out,
    time_proj,
):
    rows = memory.shape[0]
    slots = slot_rows.shape[2]
    events = src_slot.shape[1]
    core = lax.axis_index("core")

    sent, bundle = call(
        functools.partial(pack_kernel, rows),
        8,
        [
            shape((slots, BATCHES, F + 128), BF),
            shape((gru_input.shape[0], WIDE), BF),
        ],
        0,
        (
            counts[:, 0],
            slot_rows.reshape(BATCHES, slots),
            messages.reshape(BATCHES, slots, F),
            gru_input,
            gru_hidden,
            attn_qkv,
            attn_out,
            time_proj,
        ),
        "pack",
        in_specs=[VSPEC] * 3 + [HSPEC] * 5,
        out_specs=[VSPEC] * 2,
        scratch_shapes=[pltpu.SemaphoreType.DMA((8,))],
        limit=PACK_LIMIT,
    )
    near_pairs = []
    for t in range(SECTIONS):
        near_pairs.append(((t + 1) % SECTIONS * 2, t * 2))
        near_pairs.append(((t + 3) % SECTIONS * 2 + 1, t * 2 + 1))
    beside = lax.ppermute(bundle, ("section", "core"), near_pairs)
    count = gru_input.shape[0] // 2
    far = lax.ppermute(lax.dynamic_slice_in_dim(beside, core * count, count, 0), ("section", "core"), near_pairs)
    recv = lax.all_to_all(sent, SHARD, split_axis=0, concat_axis=0, tiled=True)
    swap = [(0, 1), (1, 0)]
    across = lax.ppermute(beside, "core", swap)
    recv, beside, far, across = lax.optimization_barrier((recv, beside, far, across))
    far_across = lax.ppermute(far, "core", swap)
    pieces = (bundle, beside, across, far, far_across)
    got, tail = call(
        fetch_kernel,
        2,
        [shape((2 * slots, F), BF), shape((EXTRA, F), BF)],
        3 * 10**8,
        (recv, memory),
        "fetch",
    )
    up0, gx1, w_hid = call(
        first_kernel,
        9,
        [shape((slots + EXTRA, F), BF), shape((slots, G), F32), shape((F, G), BF)],
        10**9,
        (recv, got, tail, gru_bias) + pieces,
        "first_batch",
        in_specs=[VSPEC] * 4 + [HSPEC] * 5,
        scratch_shapes=[pltpu.VMEM((F, G), BF), pltpu.SemaphoreType.DMA((2, 5))],
    )
    ups0 = lax.all_gather(up0, "section", axis=0, tiled=True)
    up1, both = call(
        functools.partial(second_kernel, float(rows)),
        7,
        [shape((slots, F), BF), shape((slots, BATCHES, F), BF)],
        3 * 10**8,
        (recv, got, ups0, gx1, up0, w_hid, gru_bias),
        "second_batch",
    )
    pools = lax.all_to_all(both, SHARD, split_axis=0, concat_axis=0, tiled=True)
    ups1 = lax.all_gather(up1, "section", axis=0, tiled=True)
    memory_out = call(
        store_kernel,
        3,
        shape((rows, F), BF),
        10**9,
        (memory, ups0, ups1),
        "store",
        grid=(4,),
        in_specs=[
            pl.BlockSpec((rows // 4, F), lambda i: (i, 0)),
            pl.BlockSpec(ups0.shape, lambda i: (0, 0)),
            pl.BlockSpec(ups1.shape, lambda i: (0, 0)),
        ],
        out_specs=pl.BlockSpec((rows // 4, F), lambda i: (i, 0)),
    )
    embeddings = call(
        attend_kernel,
        11,
        shape((BATCHES, events, F), BF),
        10**9,
        (
            pools,
            src_slot,
            nbr_slots.transpose(0, 2, 1),
            time_gap.transpose(0, 2, 1),
            time_freq.reshape(1, TE),
            time_phase.reshape(1, TE),
            *pieces,
        ),
        "attend",
        in_specs=[VSPEC] * 6 + [HSPEC] * 5,
        scratch_shapes=[
            pltpu.VMEM((F, G + F), BF),
            pltpu.VMEM((F, 256), BF),
            pltpu.VMEM((BATCHES, NBR, TE, events), BF),
            pltpu.SemaphoreType.DMA((2, 5)),
        ],
    )
    return memory_out, embeddings


def solution(mesh):
    sections, shards = mesh.devices.shape
    mesh = Mesh(mesh.devices.reshape(sections, shards // 2, 2), ALL)
    in_specs = (
        P(SHARD, None),
        P(None, SHARD, None, "section", None),
        P(None, SHARD, None, "section"),
        P(None, SHARD, None),
        P(None, ALL),
        P(None, ALL, None),
        P(None, ALL, None),
        P(),
        P(),
        P("section", None),
        P("section", None),
        P(),
        P("section", None),
        P("section", None),
        P("section", None),
    )
    out_specs = (P(SHARD, None), P(None, ALL, None))
    return jax.shard_map(body, mesh=mesh, in_specs=in_specs, out_specs=out_specs, check_vma=False)
```

```python
import functools
import math

import jax
import jax.numpy as jnp
from jax import lax
from jax.experimental import pallas as pl
from jax.experimental.pallas import tpu as pltpu
from jax.sharding import Mesh
from jax.sharding import PartitionSpec as P

HEADS = 2
HD = 256
BATCHES = 2
NBR = 10
F = 512
TE = 128
G = 3 * F
DIGIT = 32
EXTRA = 16
SHARD = ("chip", "core")
ALL = ("section", "chip", "core")
BF = jnp.bfloat16
F32 = jnp.float32
VMEM_LIMIT = 40 * 2**20
WIDE = 2 * G + G + F + 256
PACK_LIMIT = 56 * 2**20

SECTIONS = 4
HSPEC = pl.BlockSpec(memory_space=pltpu.HBM)
VSPEC = pl.BlockSpec(memory_space=pltpu.VMEM)


def dot(a, b):
    return jnp.dot(a, b, preferred_element_type=F32)


def dot_nt(a, b):
    return lax.dot_general(a, b, (((1,), (1,)), ((), ())), preferred_element_type=F32)


def dot_tn(a, b):
    return lax.dot_general(a, b, (((0,), (0,)), ((), ())), preferred_element_type=F32)


def split(x):
    high = x.astype(BF)
    return high, (x - high.astype(F32)).astype(BF)


def iota(shape, dim):
    return lax.broadcasted_iota(jnp.int32, shape, dim)


def hot(mask):
    return jnp.where(mask, 1.0, 0.0).astype(BF)


TWO_PI_HIGH = 6.28125
TWO_PI_LOW = 2.0 * math.pi - TWO_PI_HIGH
SERIES = [(-1.0) ** k / math.factorial(2 * k) for k in range(9)]


def cosine(x):
    turns = jnp.round(x * (1.0 / (2.0 * math.pi)))
    r = (x - turns * TWO_PI_HIGH) - turns * TWO_PI_LOW
    s = r * r
    y = jnp.full_like(s, SERIES[8])
    for k in range(7, -1, -1):
        y = y * s + SERIES[k]
    return y


def encode(gap, freq, phase, te):
    events = gap.shape[2]
    speed = jnp.broadcast_to(freq[...], (events, TE)).T
    start = jnp.broadcast_to(phase[...], (events, TE)).T
    for b in range(BATCHES):
        for n in range(NBR):
            te[b, n] = cosine(speed * gap[b, n : n + 1, :] + start).astype(BF)


def pack_kernel(dead, counts, wanted, messages, w_in, w_hid, w_qkv, w_out, w_time, sent, bundle, sems):
    pairs = []
    for array, at, width in [(w_in, 0, G), (w_hid, G, G), (w_qkv, 2 * G, G), (w_out, 3 * G, F)]:
        pairs.append((array, bundle.at[:, pl.ds(at, width)]))
    rows = w_time.shape[0]
    for q in range(4):
        piece = w_time.at[:, pl.ds(256 * q, 256)]
        pairs.append((piece, bundle.at[pl.ds(rows * q, rows), pl.ds(3 * G + F, 256)]))
    started = []
    for i, (source, target) in enumerate(pairs):
        copy = pltpu.make_async_copy(source, target, sems.at[i])
        copy.start()
        started.append(copy)
    number = jnp.where(counts[...] > lax.axis_index("section"), wanted[...], dead)
    high = (number // DIGIT).astype(F32)
    low = (number % DIGIT).astype(F32)
    lines = [high[0:1], low[0:1], high[1:2], low[1:2], jnp.zeros((124, number.shape[1]), F32)]
    digits = jnp.concatenate(lines, axis=0).T.astype(BF)
    for b in range(BATCHES):
        sent[:, b, :F] = messages[b]
        sent[:, b, F:] = digits
    wait(started)


def copies(pieces, col, width, target, sems):
    own, beside, across, far, far_across = pieces
    core, section = lax.axis_index("core"), lax.axis_index("section")
    count, half = own.shape[0], far.shape[0]
    turn = 1 - 2 * core
    started = []

    def put(source, step, first, length):
        where = (section + step + SECTIONS) % SECTIONS
        rows = pl.ds(pl.multiple_of(where * count + first, half), length)
        copy = pltpu.make_async_copy(source.at[:, pl.ds(col, width)], target.at[rows, :], sems.at[len(started)])
        copy.start()
        started.append(copy)

    put(own, 0, 0, count)
    put(beside, turn, 0, count)
    put(across, -turn, 0, count)
    put(far, 2, core * half, half)
    put(far_across, 2, half - core * half, half)
    return started


def wait(started):
    for copy in started:
        copy.wait()


def gates(gx, gh, h):
    reset = jax.nn.sigmoid(gx[:, :F] + gh[:, :F])
    update = jax.nn.sigmoid(gx[:, F : 2 * F] + gh[:, F : 2 * F])
    fresh = jnp.tanh(gx[:, 2 * F :] + reset * gh[:, 2 * F :])
    return ((1.0 - update) * fresh + update * h.astype(F32)).astype(BF)


def fetch_kernel(recv, memory, got, tail):
    slots = recv.shape[0]
    rows = memory.shape[0]
    digits = recv[:, 0, F:].astype(F32)
    tail[...] = jnp.zeros((EXTRA, F), BF)
    tail[:, :slots] = digits.T[:EXTRA, :].astype(BF)
    number = iota((slots, rows), 1).astype(F32)
    hot0 = hot(number == digits[:, 0:1] * DIGIT + digits[:, 1:2])
    hot1 = hot(number == digits[:, 2:3] * DIGIT + digits[:, 3:4])
    got[...] = dot(jnp.concatenate([hot0, hot1], axis=0), memory[...]).astype(BF)


def first_kernel(recv, got, tail, bias, *rest):
    pieces, (up, gx1, w_hid, w_in, sems) = rest[:5], rest[5:]
    in_copies = copies(pieces, 0, G, w_in, sems.at[0])
    hid_copies = copies(pieces, G, G, w_hid, sems.at[1])
    slots = recv.shape[0]
    up[slots:, :] = tail[...]
    sent = jnp.concatenate([recv[:, b, :F] for b in range(BATCHES)], axis=0)
    wait(in_copies)
    gx = dot(sent, w_in[...]) + bias[0:1, :]
    gx1[...] = gx[slots:]
    h = got[:slots, :]
    wait(hid_copies)
    gh = dot(h, w_hid[...]) + bias[1:2, :]
    up[:slots, :] = gates(gx[:slots], gh, h)


def numbers(ups, batch, slots):
    parts = []
    for t in range(ups.shape[0] // (slots + EXTRA)):
        at = t * (slots + EXTRA) + slots
        pair = ups[at : at + EXTRA, :slots].astype(F32)
        parts.append(pair[2 * batch : 2 * batch + 1] * DIGIT + pair[2 * batch + 1 : 2 * batch + 2])
    return jnp.concatenate(parts, axis=1)


def values(ups, slots):
    parts = []
    for t in range(ups.shape[0] // (slots + EXTRA)):
        at = t * (slots + EXTRA)
        parts.append(ups[at : at + slots, :])
    return jnp.concatenate(parts, axis=0)


def tile_order():
    to, at = iota((128, 128), 0), iota((128, 128), 1)
    return hot((at % 16) * 8 + at // 16 == to)


def second_kernel(dead, recv, got, ups, gx1, up0, w_hid, bias, up, both):
    slots = recv.shape[0]
    digits = recv[:, 0, F:].astype(F32)
    mine = digits[:, 2:3] * DIGIT + digits[:, 3:4]
    same = (numbers(ups, 0, slots) == mine) & (mine < dead)
    any_same = jnp.max(jnp.where(same, 1.0, 0.0), axis=1, keepdims=True)
    moved = dot(hot(same), values(ups, slots))
    h = jnp.where(any_same > 0.0, moved, got[slots:, :].astype(F32)).astype(BF)
    gh = dot(h, w_hid[...]) + bias[1:2, :]
    new = gates(gx1[...], gh, h)
    up[...] = new
    order = tile_order()
    for i in range(slots // 16):
        at = slice(16 * i, 16 * i + 16)
        lines = [up0[at, 128 * c : 128 * c + 128] for c in range(4)]
        lines += [new[at, 128 * c : 128 * c + 128] for c in range(4)]
        both[128 * i : 128 * i + 128, :] = dot(order, jnp.concatenate(lines, axis=0)).astype(BF)


def store_kernel(memory, ups0, ups1, out):
    block = memory.shape[0]
    slots = ups0.shape[0] // SECTIONS - EXTRA
    number = (iota((block, 1), 0) + pl.program_id(0) * block).astype(F32)
    hot0 = hot(numbers(ups0, 0, slots) == number)
    hot1 = hot(numbers(ups0, 1, slots) == number)
    ones = jnp.ones((hot0.shape[1], 128), BF)
    seen0, seen1 = dot(hot0, ones), dot(hot1, ones)
    new0 = dot(hot0, values(ups0, slots))
    new1 = dot(hot1, ups1[...])
    for c in range(0, F, 128):
        cols = slice(c, c + 128)
        old = jnp.where(seen0 > 0.0, new0[:, cols], memory[:, cols].astype(F32))
        out[:, cols] = jnp.where(seen1 > 0.0, new1[:, cols], old).astype(BF)


def place_kernel(*refs):
    pieces, (w, w_late, sems) = refs[:5], refs[5:]
    wait(copies(pieces, 2 * G, G, w, sems.at[0]) + copies(pieces, 3 * G, F + 256, w_late, sems.at[1]))


def attend_kernel(pools, source, nearby, gap, freq, phase, w, w_late, out, te):
    slots = pools.shape[0] // 8
    events = source.shape[1]
    number = iota((slots, events), 0)
    order = tile_order()
    lines = [[] for _ in range(BATCHES)]
    for i in range(slots // 16):
        block = dot_tn(order, pools[128 * i : 128 * i + 128, :]).astype(BF)
        for b in range(BATCHES):
            parts = [block[64 * b + 16 * c : 64 * b + 16 * c + 16] for c in range(4)]
            lines[b].append(jnp.concatenate(parts, axis=1))
    pool = [jnp.concatenate(lines[b], axis=0) for b in range(BATCHES)]
    picked = [dot_tn(hot(number == source[b : b + 1, :]), pool[b]).astype(BF) for b in range(BATCHES)]
    encode(gap, freq, phase, te)
    kv = dot(jnp.concatenate(pool, axis=0), w[:, F:]).astype(BF)
    query = dot(jnp.concatenate(picked, axis=0), w[:, :F]) * (1.0 / math.sqrt(HD))
    quarter = w_late.shape[0] // SECTIONS
    w_time = [
        jnp.concatenate([w_late[t * quarter + 32 * q : t * quarter + 32 * q + 32, F:] for t in range(SECTIONS)], axis=0)
        for q in range(2 * HEADS)
    ]
    mixed = []
    for b in range(BATCHES):
        hits = [number == nearby[b, n : n + 1, :] for n in range(NBR)]
        pieces_of = []
        for head in range(HEADS):
            cols = slice(head * HD, (head + 1) * HD)
            vcols = slice(F + head * HD, F + (head + 1) * HD)
            own = slice(b * slots, (b + 1) * slots)
            high, low = split(query[b * events : (b + 1) * events, cols])
            keys = jnp.concatenate([kv[own, cols], w_time[head]], axis=0)
            twice = dot_nt(keys, jnp.concatenate([high, low], axis=0))
            product = twice[:, :events] + twice[:, events:]
            by_slot, by_time = product[:slots], product[slots:]
            scores = [
                jnp.sum(
                    jnp.where(hits[n], by_slot, 0.0) + by_time * te[b, n].astype(F32),
                    axis=0,
                    keepdims=True,
                )
                for n in range(NBR)
            ]
            top = functools.reduce(jnp.maximum, scores)
            grown = [jnp.exp(s - top) for s in scores]
            scale = 1.0 / functools.reduce(jnp.add, grown)
            on_slot = jnp.zeros((slots, events), F32)
            on_time = jnp.zeros((TE, events), F32)
            for n in range(NBR):
                weight = grown[n] * scale
                on_slot = on_slot + jnp.where(hits[n], weight, 0.0)
                on_time = on_time + te[b, n].astype(F32) * weight
            w_high, w_low = split(jnp.concatenate([on_slot, on_time], axis=0))
            found = jnp.concatenate([kv[own, vcols], w_time[HEADS + head]], axis=0)
            twice = dot_tn(jnp.concatenate([w_high, w_low], axis=1), found)
            pieces_of.append(twice[:events] + twice[events:])
        mixed.append(jnp.concatenate(pieces_of, axis=1).astype(BF))
    result = dot(jnp.concatenate(mixed, axis=0), w_late[:, :F]).astype(BF)
    for b in range(BATCHES):
        out[b] = result[b * events : (b + 1) * events]


def call(kernel, n_in, outs, flops, args, name, **more):
    many = isinstance(outs, (list, tuple))
    moved = sum(a.size * a.dtype.itemsize for a in args)
    return pl.pallas_call(
        kernel,
        out_shape=outs,
        in_specs=more.pop("in_specs", [VSPEC] * n_in),
        out_specs=more.pop("out_specs", [VSPEC] * len(outs) if many else VSPEC),
        compiler_params=pltpu.CompilerParams(vmem_limit_bytes=more.pop("limit", VMEM_LIMIT)),
        cost_estimate=pl.CostEstimate(flops=flops, bytes_accessed=moved, transcendentals=0),
        name=name,
        **more,
    )(*args)


def shape(dims, kind):
    return jax.ShapeDtypeStruct(dims, kind)


def body(
    memory,
    messages,
    slot_rows,
    counts,
    src_slot,
    nbr_slots,
    time_gap,
    time_freq,
    time_phase,
    gru_input,
    gru_hidden,
    gru_bias,
    attn_qkv,
    attn_out,
    time_proj,
):
    rows = memory.shape[0]
    slots = slot_rows.shape[2]
    events = src_slot.shape[1]
    core = lax.axis_index("core")

    sent, bundle = call(
        functools.partial(pack_kernel, rows),
        8,
        [
            shape((slots, BATCHES, F + 128), BF),
            shape((gru_input.shape[0], WIDE), BF),
        ],
        0,
        (
            counts[:, 0],
            slot_rows.reshape(BATCHES, slots),
            messages.reshape(BATCHES, slots, F),
            gru_input,
            gru_hidden,
            attn_qkv,
            attn_out,
            time_proj,
        ),
        "pack",
        in_specs=[VSPEC] * 3 + [HSPEC] * 5,
        out_specs=[VSPEC] * 2,
        scratch_shapes=[pltpu.SemaphoreType.DMA((8,))],
        limit=PACK_LIMIT,
    )
    near_pairs = []
    for t in range(SECTIONS):
        near_pairs.append(((t + 1) % SECTIONS * 2, t * 2))
        near_pairs.append(((t + 3) % SECTIONS * 2 + 1, t * 2 + 1))
    beside = lax.ppermute(bundle, ("section", "core"), near_pairs)
    count = gru_input.shape[0] // 2
    far = lax.ppermute(lax.dynamic_slice_in_dim(beside, core * count, count, 0), ("section", "core"), near_pairs)
    recv = lax.all_to_all(sent, SHARD, split_axis=0, concat_axis=0, tiled=True)
    swap = [(0, 1), (1, 0)]
    across = lax.ppermute(beside, "core", swap)
    recv, beside, far, across = lax.optimization_barrier((recv, beside, far, across))
    far_across = lax.ppermute(far, "core", swap)
    pieces = (bundle, beside, across, far, far_across)
    got, tail = call(
        fetch_kernel,
        2,
        [shape((2 * slots, F), BF), shape((EXTRA, F), BF)],
        3 * 10**8,
        (recv, memory),
        "fetch",
    )
    up0, gx1, w_hid = call(
        first_kernel,
        9,
        [shape((slots + EXTRA, F), BF), shape((slots, G), F32), shape((F, G), BF)],
        10**9,
        (recv, got, tail, gru_bias) + pieces,
        "first_batch",
        in_specs=[VSPEC] * 4 + [HSPEC] * 5,
        scratch_shapes=[pltpu.VMEM((F, G), BF), pltpu.SemaphoreType.DMA((2, 5))],
    )
    ups0 = lax.all_gather(up0, "section", axis=0, tiled=True)
    up1, both = call(
        functools.partial(second_kernel, float(rows)),
        7,
        [shape((slots, F), BF), shape((slots * 8, 128), BF)],
        3 * 10**8,
        (recv, got, ups0, gx1, up0, w_hid, gru_bias),
        "second_batch",
    )
    pools = lax.all_to_all(both, SHARD, split_axis=0, concat_axis=0, tiled=True)
    ups1 = lax.all_gather(up1, "section", axis=0, tiled=True)
    memory_out = call(
        store_kernel,
        3,
        shape((rows, F), BF),
        10**9,
        (memory, ups0, ups1),
        "store",
        grid=(4,),
        in_specs=[
            pl.BlockSpec((rows // 4, F), lambda i: (i, 0)),
            pl.BlockSpec(ups0.shape, lambda i: (0, 0)),
            pl.BlockSpec(ups1.shape, lambda i: (0, 0)),
        ],
        out_specs=pl.BlockSpec((rows // 4, F), lambda i: (i, 0)),
    )
    w, w_late = call(
        place_kernel,
        5,
        [shape((F, G), BF), shape((F, F + 256), BF)],
        0,
        pieces,
        "place",
        in_specs=[HSPEC] * 5,
        scratch_shapes=[pltpu.SemaphoreType.DMA((2, 5))],
    )
    embeddings = call(
        attend_kernel,
        8,
        shape((BATCHES, events, F), BF),
        10**9,
        (
            pools,
            src_slot,
            nbr_slots.transpose(0, 2, 1),
            time_gap.transpose(0, 2, 1),
            time_freq.reshape(1, TE),
            time_phase.reshape(1, TE),
            w,
            w_late,
        ),
        "attend",
        scratch_shapes=[
            pltpu.VMEM((BATCHES, NBR, TE, events), BF),
        ],
    )
    return memory_out, embeddings


def solution(mesh):
    sections, shards = mesh.devices.shape
    mesh = Mesh(mesh.devices.reshape(sections, shards // 2, 2), ALL)
    in_specs = (
        P(SHARD, None),
        P(None, SHARD, None, "section", None),
        P(None, SHARD, None, "section"),
        P(None, SHARD, None),
        P(None, ALL),
        P(None, ALL, None),
        P(None, ALL, None),
        P(),
        P(),
        P("section", None),
        P("section", None),
        P(),
        P("section", None),
        P("section", None),
        P("section", None),
    )
    out_specs = (P(SHARD, None), P(None, ALL, None))
    return jax.shard_map(body, mesh=mesh, in_specs=in_specs, out_specs=out_specs, check_vma=False)
```

```python
import functools
import math

import jax
import jax.numpy as jnp
from jax import lax
from jax.experimental import pallas as pl
from jax.experimental.pallas import tpu as pltpu
from jax.sharding import Mesh
from jax.sharding import PartitionSpec as P

HEADS = 2
HD = 256
BATCHES = 2
NBR = 10
F = 512
TE = 128
G = 3 * F
DIGIT = 32
EXTRA = 16
SHARD = ("chip", "core")
ALL = ("section", "chip", "core")
BF = jnp.bfloat16
F32 = jnp.float32
VMEM_LIMIT = 40 * 2**20
WIDE = 2 * G + G + F + 256
PACK_LIMIT = 56 * 2**20

SECTIONS = 4
HSPEC = pl.BlockSpec(memory_space=pltpu.HBM)
VSPEC = pl.BlockSpec(memory_space=pltpu.VMEM)


def dot(a, b):
    return jnp.dot(a, b, preferred_element_type=F32)


def dot_nt(a, b):
    return lax.dot_general(a, b, (((1,), (1,)), ((), ())), preferred_element_type=F32)


def dot_tn(a, b):
    return lax.dot_general(a, b, (((0,), (0,)), ((), ())), preferred_element_type=F32)


def split(x):
    high = x.astype(BF)
    return high, (x - high.astype(F32)).astype(BF)


def iota(shape, dim):
    return lax.broadcasted_iota(jnp.int32, shape, dim)


def hot(mask):
    return jnp.where(mask, 1.0, 0.0).astype(BF)


TWO_PI_HIGH = 6.28125
TWO_PI_LOW = 2.0 * math.pi - TWO_PI_HIGH
SERIES = [(-1.0) ** k / math.factorial(2 * k) for k in range(9)]


def cosine(x):
    turns = jnp.round(x * (1.0 / (2.0 * math.pi)))
    r = (x - turns * TWO_PI_HIGH) - turns * TWO_PI_LOW
    s = r * r
    y = jnp.full_like(s, SERIES[8])
    for k in range(7, -1, -1):
        y = y * s + SERIES[k]
    return y


def encode(gap, freq, phase, te):
    events = gap.shape[2]
    speed = jnp.broadcast_to(freq[...], (events, TE)).T
    start = jnp.broadcast_to(phase[...], (events, TE)).T
    for b in range(BATCHES):
        for n in range(NBR):
            te[b, n] = cosine(speed * gap[b, n : n + 1, :] + start).astype(BF)


def pack_kernel(dead, counts, wanted, messages, w_in, w_hid, w_qkv, w_out, w_time, sent, bundle, sems):
    pairs = []
    for array, at, width in [(w_in, 0, G), (w_hid, G, G), (w_qkv, 2 * G, G), (w_out, 3 * G, F)]:
        pairs.append((array, bundle.at[:, pl.ds(at, width)]))
    rows = w_time.shape[0]
    for q in range(4):
        piece = w_time.at[:, pl.ds(256 * q, 256)]
        pairs.append((piece, bundle.at[pl.ds(rows * q, rows), pl.ds(3 * G + F, 256)]))
    started = []
    for i, (source, target) in enumerate(pairs):
        copy = pltpu.make_async_copy(source, target, sems.at[i])
        copy.start()
        started.append(copy)
    number = jnp.where(counts[...] > lax.axis_index("section"), wanted[...], dead)
    high = (number // DIGIT).astype(F32)
    low = (number % DIGIT).astype(F32)
    lines = [high[0:1], low[0:1], high[1:2], low[1:2], jnp.zeros((124, number.shape[1]), F32)]
    digits = jnp.concatenate(lines, axis=0).T.astype(BF)
    for b in range(BATCHES):
        sent[:, b, :F] = messages[b]
        sent[:, b, F:] = digits
    wait(started)


def copies(pieces, col, width, target, sems):
    own, beside, across, far, far_across = pieces
    core, section = lax.axis_index("core"), lax.axis_index("section")
    count, half = own.shape[0], far.shape[0]
    turn = 1 - 2 * core
    started = []

    def put(source, step, first, length):
        where = (section + step + SECTIONS) % SECTIONS
        rows = pl.ds(pl.multiple_of(where * count + first, half), length)
        copy = pltpu.make_async_copy(source.at[:, pl.ds(col, width)], target.at[rows, :], sems.at[len(started)])
        copy.start()
        started.append(copy)

    put(own, 0, 0, count)
    put(beside, turn, 0, count)
    put(across, -turn, 0, count)
    put(far, 2, core * half, half)
    put(far_across, 2, half - core * half, half)
    return started


def wait(started):
    for copy in started:
        copy.wait()


def gates(gx, gh, h):
    reset = jax.nn.sigmoid(gx[:, :F] + gh[:, :F])
    update = jax.nn.sigmoid(gx[:, F : 2 * F] + gh[:, F : 2 * F])
    fresh = jnp.tanh(gx[:, 2 * F :] + reset * gh[:, 2 * F :])
    return ((1.0 - update) * fresh + update * h.astype(F32)).astype(BF)


def first_kernel(recv, memory, bias, *rest):
    pieces, (up, got, gx1, w_hid, w_in, sems) = rest[:5], rest[5:]
    in_copies = copies(pieces, 0, G, w_in, sems.at[0])
    hid_copies = copies(pieces, G, G, w_hid, sems.at[1])
    slots = recv.shape[0]
    rows = memory.shape[0]
    digits = recv[:, 0, F:].astype(F32)
    up[slots:, :] = jnp.zeros((EXTRA, F), BF)
    up[slots:, :slots] = digits.T[:EXTRA, :].astype(BF)
    number = iota((slots, rows), 1).astype(F32)
    hot0 = hot(number == digits[:, 0:1] * DIGIT + digits[:, 1:2])
    hot1 = hot(number == digits[:, 2:3] * DIGIT + digits[:, 3:4])
    got[...] = dot(jnp.concatenate([hot0, hot1], axis=0), memory[...]).astype(BF)
    sent = jnp.concatenate([recv[:, b, :F] for b in range(BATCHES)], axis=0)
    wait(in_copies)
    gx = dot(sent, w_in[...]) + bias[0:1, :]
    gx1[...] = gx[slots:]
    h = got[:slots, :]
    wait(hid_copies)
    gh = dot(h, w_hid[...]) + bias[1:2, :]
    up[:slots, :] = gates(gx[:slots], gh, h)


def numbers(ups, batch, slots):
    parts = []
    for t in range(ups.shape[0] // (slots + EXTRA)):
        at = t * (slots + EXTRA) + slots
        pair = ups[at : at + EXTRA, :slots].astype(F32)
        parts.append(pair[2 * batch : 2 * batch + 1] * DIGIT + pair[2 * batch + 1 : 2 * batch + 2])
    return jnp.concatenate(parts, axis=1)


def values(ups, slots):
    parts = []
    for t in range(ups.shape[0] // (slots + EXTRA)):
        at = t * (slots + EXTRA)
        parts.append(ups[at : at + slots, :])
    return jnp.concatenate(parts, axis=0)


def tile_order():
    to, at = iota((128, 128), 0), iota((128, 128), 1)
    return hot((at % 16) * 8 + at // 16 == to)


def second_kernel(dead, recv, got, ups, gx1, up0, w_hid, bias, up, both):
    slots = recv.shape[0]
    digits = recv[:, 0, F:].astype(F32)
    mine = digits[:, 2:3] * DIGIT + digits[:, 3:4]
    same = (numbers(ups, 0, slots) == mine) & (mine < dead)
    any_same = jnp.max(jnp.where(same, 1.0, 0.0), axis=1, keepdims=True)
    moved = dot(hot(same), values(ups, slots))
    h = jnp.where(any_same > 0.0, moved, got[slots:, :].astype(F32)).astype(BF)
    gh = dot(h, w_hid[...]) + bias[1:2, :]
    new = gates(gx1[...], gh, h)
    up[...] = new
    order = tile_order()
    for i in range(slots // 16):
        at = slice(16 * i, 16 * i + 16)
        lines = [up0[at, 128 * c : 128 * c + 128] for c in range(4)]
        lines += [new[at, 128 * c : 128 * c + 128] for c in range(4)]
        both[128 * i : 128 * i + 128, :] = dot(order, jnp.concatenate(lines, axis=0)).astype(BF)


def store_kernel(memory, ups0, ups1, out):
    block = memory.shape[0]
    slots = ups0.shape[0] // SECTIONS - EXTRA
    number = (iota((block, 1), 0) + pl.program_id(0) * block).astype(F32)
    hot0 = hot(numbers(ups0, 0, slots) == number)
    hot1 = hot(numbers(ups0, 1, slots) == number)
    ones = jnp.ones((hot0.shape[1], 128), BF)
    seen0, seen1 = dot(hot0, ones), dot(hot1, ones)
    new0 = dot(hot0, values(ups0, slots))
    new1 = dot(hot1, ups1[...])
    for c in range(0, F, 128):
        cols = slice(c, c + 128)
        old = jnp.where(seen0 > 0.0, new0[:, cols], memory[:, cols].astype(F32))
        out[:, cols] = jnp.where(seen1 > 0.0, new1[:, cols], old).astype(BF)


def place_kernel(*refs):
    pieces, (w, w_late, sems) = refs[:5], refs[5:]
    wait(copies(pieces, 2 * G, G, w, sems.at[0]) + copies(pieces, 3 * G, F + 256, w_late, sems.at[1]))


def attend_kernel(pools, source, nearby, gap, freq, phase, w, w_late, out, te):
    slots = pools.shape[0] // 8
    events = source.shape[1]
    number = iota((slots, events), 0)
    order = tile_order()
    lines = [[] for _ in range(BATCHES)]
    for i in range(slots // 16):
        block = dot_tn(order, pools[128 * i : 128 * i + 128, :]).astype(BF)
        for b in range(BATCHES):
            parts = [block[64 * b + 16 * c : 64 * b + 16 * c + 16] for c in range(4)]
            lines[b].append(jnp.concatenate(parts, axis=1))
    pool = [jnp.concatenate(lines[b], axis=0) for b in range(BATCHES)]
    picked = [dot_tn(hot(number == source[b : b + 1, :]), pool[b]).astype(BF) for b in range(BATCHES)]
    encode(gap, freq, phase, te)
    kv = dot(jnp.concatenate(pool, axis=0), w[:, F:]).astype(BF)
    query = dot(jnp.concatenate(picked, axis=0), w[:, :F]) * (1.0 / math.sqrt(HD))
    quarter = w_late.shape[0] // SECTIONS
    w_time = [
        jnp.concatenate([w_late[t * quarter + 32 * q : t * quarter + 32 * q + 32, F:] for t in range(SECTIONS)], axis=0)
        for q in range(2 * HEADS)
    ]
    mixed = []
    for b in range(BATCHES):
        hits = [number == nearby[b, n : n + 1, :] for n in range(NBR)]
        pieces_of = []
        for head in range(HEADS):
            cols = slice(head * HD, (head + 1) * HD)
            vcols = slice(F + head * HD, F + (head + 1) * HD)
            own = slice(b * slots, (b + 1) * slots)
            high, low = split(query[b * events : (b + 1) * events, cols])
            keys = jnp.concatenate([kv[own, cols], w_time[head]], axis=0)
            twice = dot_nt(keys, jnp.concatenate([high, low], axis=0))
            product = twice[:, :events] + twice[:, events:]
            by_slot, by_time = product[:slots], product[slots:]
            scores = [
                jnp.sum(
                    jnp.where(hits[n], by_slot, 0.0) + by_time * te[b, n].astype(F32),
                    axis=0,
                    keepdims=True,
                )
                for n in range(NBR)
            ]
            top = functools.reduce(jnp.maximum, scores)
            grown = [jnp.exp(s - top) for s in scores]
            scale = 1.0 / functools.reduce(jnp.add, grown)
            on_slot = jnp.zeros((slots, events), F32)
            on_time = jnp.zeros((TE, events), F32)
            for n in range(NBR):
                weight = grown[n] * scale
                on_slot = on_slot + jnp.where(hits[n], weight, 0.0)
                on_time = on_time + te[b, n].astype(F32) * weight
            w_high, w_low = split(jnp.concatenate([on_slot, on_time], axis=0))
            found = jnp.concatenate([kv[own, vcols], w_time[HEADS + head]], axis=0)
            twice = dot_tn(jnp.concatenate([w_high, w_low], axis=1), found)
            pieces_of.append(twice[:events] + twice[events:])
        mixed.append(jnp.concatenate(pieces_of, axis=1).astype(BF))
    result = dot(jnp.concatenate(mixed, axis=0), w_late[:, :F]).astype(BF)
    for b in range(BATCHES):
        out[b] = result[b * events : (b + 1) * events]


def call(kernel, n_in, outs, flops, args, name, **more):
    many = isinstance(outs, (list, tuple))
    moved = sum(a.size * a.dtype.itemsize for a in args)
    return pl.pallas_call(
        kernel,
        out_shape=outs,
        in_specs=more.pop("in_specs", [VSPEC] * n_in),
        out_specs=more.pop("out_specs", [VSPEC] * len(outs) if many else VSPEC),
        compiler_params=pltpu.CompilerParams(vmem_limit_bytes=more.pop("limit", VMEM_LIMIT)),
        cost_estimate=pl.CostEstimate(flops=flops, bytes_accessed=moved, transcendentals=0),
        name=name,
        **more,
    )(*args)


def shape(dims, kind):
    return jax.ShapeDtypeStruct(dims, kind)


def body(
    memory,
    messages,
    slot_rows,
    counts,
    src_slot,
    nbr_slots,
    time_gap,
    time_freq,
    time_phase,
    gru_input,
    gru_hidden,
    gru_bias,
    attn_qkv,
    attn_out,
    time_proj,
):
    rows = memory.shape[0]
    slots = slot_rows.shape[2]
    events = src_slot.shape[1]
    core = lax.axis_index("core")

    sent, bundle = call(
        functools.partial(pack_kernel, rows),
        8,
        [
            shape((slots, BATCHES, F + 128), BF),
            shape((gru_input.shape[0], WIDE), BF),
        ],
        0,
        (
            counts[:, 0],
            slot_rows.reshape(BATCHES, slots),
            messages.reshape(BATCHES, slots, F),
            gru_input,
            gru_hidden,
            attn_qkv,
            attn_out,
            time_proj,
        ),
        "pack",
        in_specs=[VSPEC] * 3 + [HSPEC] * 5,
        out_specs=[VSPEC] * 2,
        scratch_shapes=[pltpu.SemaphoreType.DMA((8,))],
        limit=PACK_LIMIT,
    )
    near_pairs = []
    for t in range(SECTIONS):
        near_pairs.append(((t + 1) % SECTIONS * 2, t * 2))
        near_pairs.append(((t + 3) % SECTIONS * 2 + 1, t * 2 + 1))
    beside = lax.ppermute(bundle, ("section", "core"), near_pairs)
    count = gru_input.shape[0] // 2
    far = lax.ppermute(lax.dynamic_slice_in_dim(beside, core * count, count, 0), ("section", "core"), near_pairs)
    recv = lax.all_to_all(sent, SHARD, split_axis=0, concat_axis=0, tiled=True)
    swap = [(0, 1), (1, 0)]
    across = lax.ppermute(beside, "core", swap)
    recv, beside, far, across = lax.optimization_barrier((recv, beside, far, across))
    far_across = lax.ppermute(far, "core", swap)
    pieces = (bundle, beside, across, far, far_across)
    up0, got, gx1, w_hid = call(
        first_kernel,
        8,
        [
            shape((slots + EXTRA, F), BF),
            shape((2 * slots, F), BF),
            shape((slots, G), F32),
            shape((F, G), BF),
        ],
        10**9,
        (recv, memory, gru_bias) + pieces,
        "first_batch",
        in_specs=[VSPEC] * 3 + [HSPEC] * 5,
        scratch_shapes=[pltpu.VMEM((F, G), BF), pltpu.SemaphoreType.DMA((2, 5))],
    )
    ups0 = lax.all_gather(up0, "section", axis=0, tiled=True)
    up1, both = call(
        functools.partial(second_kernel, float(rows)),
        7,
        [shape((slots, F), BF), shape((slots * 8, 128), BF)],
        3 * 10**8,
        (recv, got, ups0, gx1, up0, w_hid, gru_bias),
        "second_batch",
    )
    pools = lax.all_to_all(both, SHARD, split_axis=0, concat_axis=0, tiled=True)
    ups1 = lax.all_gather(up1, "section", axis=0, tiled=True)
    memory_out = call(
        store_kernel,
        3,
        shape((rows, F), BF),
        10**9,
        (memory, ups0, ups1),
        "store",
        grid=(4,),
        in_specs=[
            pl.BlockSpec((rows // 4, F), lambda i: (i, 0)),
            pl.BlockSpec(ups0.shape, lambda i: (0, 0)),
            pl.BlockSpec(ups1.shape, lambda i: (0, 0)),
        ],
        out_specs=pl.BlockSpec((rows // 4, F), lambda i: (i, 0)),
    )
    w, w_late = call(
        place_kernel,
        5,
        [shape((F, G), BF), shape((F, F + 256), BF)],
        0,
        pieces,
        "place",
        in_specs=[HSPEC] * 5,
        scratch_shapes=[pltpu.SemaphoreType.DMA((2, 5))],
    )
    embeddings = call(
        attend_kernel,
        8,
        shape((BATCHES, events, F), BF),
        10**9,
        (
            pools,
            src_slot,
            nbr_slots.transpose(0, 2, 1),
            time_gap.transpose(0, 2, 1),
            time_freq.reshape(1, TE),
            time_phase.reshape(1, TE),
            w,
            w_late,
        ),
        "attend",
        scratch_shapes=[
            pltpu.VMEM((BATCHES, NBR, TE, events), BF),
        ],
    )
    return memory_out, embeddings


def solution(mesh):
    sections, shards = mesh.devices.shape
    mesh = Mesh(mesh.devices.reshape(sections, shards // 2, 2), ALL)
    in_specs = (
        P(SHARD, None),
        P(None, SHARD, None, "section", None),
        P(None, SHARD, None, "section"),
        P(None, SHARD, None),
        P(None, ALL),
        P(None, ALL, None),
        P(None, ALL, None),
        P(),
        P(),
        P("section", None),
        P("section", None),
        P(),
        P("section", None),
        P("section", None),
        P("section", None),
    )
    out_specs = (P(SHARD, None), P(None, ALL, None))
    return jax.shard_map(body, mesh=mesh, in_specs=in_specs, out_specs=out_specs, check_vma=False)
```
